256 devices in a mesh: rep: 32 (over x, y, core), node: 8 (over z).
Axes of the slice: x: 4, y: 4, z: 8, core: 2. Of those that a mesh axis runs over, the one named last changes fastest.
Arguments:
- attn_out: bfloat16 [32, 2560, 2048], P('rep', 'node'), may hold values from -0.125 to 0.125
- out_grad: bfloat16 [32, 2560, 3968], P('rep', 'node'), may hold values from -6 to 6
- weight: bfloat16 [2048, 3968], P('node'), may hold values from -0.09375 to 0.09375
- error: bfloat16 [32, 2048, 3968], P('rep', 'node'), may hold values from -6 to 6
- q_prev: float32 [8, 32, 3968], P('node'), may hold values from -6 to 6
Outputs:
- input_grad: bfloat16 [32, 2560, 2048], P('rep', 'node')
- new_error: bfloat16 [32, 2048, 3968], P('rep', 'node')
- p_out: float32 [32, 2048], P(None, 'node')
- q_out: float32 [8, 32, 3968], P('node')
The draws below stay inside these ranges and needn't reach their ends.
All inputs are finite; a program needn't handle non-finite values.
Results may differ from the reference program's by a relative error of at most 0.00055.
Values may be sent and summed in bfloat16 or wider, within the bound.
A program may use at most 192 MiB of HBM per device.

```python
import jax
import jax.numpy as jnp
from jax import lax

D = 3968
RANK = 32
TOK_DEV = 320
HD = 2048
ROWS = 2560
REPLICAS = 32
SHARDS = 8
N_REP = 32
N_NODE = 8


def steps_of(rng, dims, split, low, largest):
    level = 1.0
    for axis_at, shards_of in split:
        draws = jax.random.uniform(jax.random.fold_in(jax.random.fold_in(rng, 6), axis_at), (shards_of,), jnp.float32, low / len(split), largest / len(split))
        level = level * jnp.repeat(jnp.exp(draws), dims[axis_at] // shards_of).reshape((-1,) + (1,) * (len(dims) - 1 - axis_at))
    return level


def bell_draw(stream_key, dims, deviation, reach, shards=(), dtype=jnp.bfloat16):
    drawn = deviation * jax.random.normal(stream_key, dims, jnp.float32)
    if shards:
        drawn = drawn * steps_of(stream_key, dims, shards, -0.22, 0.18)
    return jnp.clip(drawn, -reach, reach).astype(dtype)


def setup_inputs(seed: int = 0) -> dict:
    arg_keys = jax.random.split(jax.random.key(seed), 6)
    return {
        "attn_out": bell_draw(arg_keys[0], (REPLICAS, ROWS, HD), ((N_NODE * TOK_DEV) ** -0.5), 0.125, ((0, 32), (1, 8))),
        "out_grad": bell_draw(arg_keys[1], (REPLICAS, ROWS, D), 1.0, 6.0, ((0, 32), (1, 8))),
        "weight": bell_draw(arg_keys[2], (HD, D), D ** -0.5, 0.09375, ((0, 8),)),
        "error": bell_draw(arg_keys[3], (REPLICAS, HD, D), 1.0, 6.0, ((0, 32), (1, 8))),
        "q_prev": bell_draw(arg_keys[4], (SHARDS, RANK, D), 1.0, 6.0, ((0, 8),), jnp.float32),
    }


def reference(attn_out, out_grad, weight, error, q_prev):
    shard_rows = HD // N_NODE
    highest = lax.Precision.HIGHEST

    def one_replica(items):
        feats, cotan, memo = items
        back = jnp.dot(cotan.astype(jnp.float32), weight.T.astype(jnp.float32), preferred_element_type=jnp.float32).astype(jnp.bfloat16)
        feat_blocks = feats.reshape(N_NODE, TOK_DEV, HD).astype(jnp.float32)
        cotan_blocks = cotan.reshape(N_NODE, TOK_DEV, D).astype(jnp.float32)
        partial_value = jnp.einsum('ntk,ntd->nkd', feat_blocks, cotan_blocks, precision=highest)
        grad = jnp.sum(partial_value, axis=0)
        return (back, grad + memo.astype(jnp.float32))
    input_grad, memory = lax.map(one_replica, (attn_out, out_grad, error))
    memory = memory.reshape(N_REP, N_NODE, shard_rows, D)
    left = jnp.einsum('rjhd,jkd->jkh', memory, q_prev, precision=highest)
    gram = jnp.einsum('jkh,jlh->jkl', left, left, precision=highest)
    lower_factor = jnp.linalg.cholesky(gram)
    basis = jax.scipy.linalg.solve_triangular(lower_factor, left, lower=True)
    right = jnp.einsum('rjhd,jkh->jkd', memory, basis, precision=highest) / N_REP
    approx = jnp.einsum('jkh,jkd->jhd', basis, right, precision=highest)
    new_error = (memory - approx[None]).reshape(N_REP, HD, D).astype(jnp.bfloat16)
    p_out = jnp.transpose(basis, (1, 0, 2)).reshape(RANK, HD)
    return (input_grad, new_error, p_out, right)
```

```python
import functools

import jax
import jax.numpy as jnp
from jax import lax
from jax.experimental import pallas as pl
from jax.experimental.pallas import tpu as pltpu
from jax.sharding import PartitionSpec as P

MESH = pl.DeviceIdType.MESH
NODES = 8
TOK = 320
SHARD = 256
D = 3968
WIDTHS = (512, 512, 512, 512, 512, 512, 512, 384)
STARTS = tuple(sum(WIDTHS[:i]) for i in range(len(WIDTHS)))
CHUNKS = len(WIDTHS)
HALF = TOK // 2


def gather_kernel(
    a_ref, g_ref, err_ref, mem_ref,
    gbuf, abuf, at, errbuf,
    asend, arecv, gsend, grecv, lsem,
):
    me = lax.axis_index("node")

    def peer(d):
        return lax.rem(me + d + NODES, NODES)

    barrier = pltpu.get_barrier_semaphore()
    for d in range(1, NODES):
        pl.semaphore_signal(barrier, inc=1, device_id={"node": peer(d)}, device_id_type=MESH)
    own_g = pltpu.make_async_copy(g_ref, gbuf.at[me], lsem.at[0])
    own_g.start()
    own_a = pltpu.make_async_copy(
        a_ref.at[:, pl.ds(pl.multiple_of(me * SHARD, SHARD), SHARD)], abuf.at[me], lsem.at[1]
    )
    own_a.start()
    own_e = pltpu.make_async_copy(err_ref, errbuf, lsem.at[2])
    own_e.start()
    pl.semaphore_wait(barrier, NODES - 1)

    def a_copy(d, slot):
        to = peer(d)
        return pltpu.make_async_remote_copy(
            src_ref=a_ref.at[:, pl.ds(pl.multiple_of(to * SHARD, SHARD), SHARD)],
            dst_ref=abuf.at[slot],
            send_sem=asend.at[d],
            recv_sem=arecv.at[d],
            device_id={"node": to},
            device_id_type=MESH,
        )

    def g_copy(way, chunk, hop, source):
        rows = pl.ds(0, TOK) if hop < 3 else pl.ds(0 if way == 0 else HALF, HALF)
        cols = pl.ds(STARTS[chunk], WIDTHS[chunk])
        src = g_ref.at[:, cols] if hop == 0 else gbuf.at[source, rows, cols]
        return pltpu.make_async_remote_copy(
            src_ref=src,
            dst_ref=gbuf.at[source, rows, cols],
            send_sem=gsend.at[way, chunk, hop],
            recv_sem=grecv.at[way, chunk, hop],
            device_id={"node": peer(1 if way == 0 else -1)},
            device_id_type=MESH,
        )

    def behind(way, n):
        return peer(-n if way == 0 else n)

    for d in (4, 3, 5, 2, 6, 1, 7):
        a_copy(d, me).start()

    def compute(chunk):
        cols = pl.ds(STARTS[chunk], WIDTHS[chunk])
        block = gbuf[:, :, cols].reshape(NODES * TOK, WIDTHS[chunk])
        grad = jnp.dot(at[...], block, preferred_element_type=jnp.float32)
        mem_ref[:, cols] = grad + errbuf[:, cols].astype(jnp.float32)

    for t in range(CHUNKS + 4):
        for hop in range(4):
            chunk = t - hop
            if 0 <= chunk < CHUNKS:
                for way in range(2):
                    if hop:
                        g_copy(way, chunk, hop - 1, behind(way, hop)).wait_recv()
                    g_copy(way, chunk, hop, behind(way, hop)).start()
        if t == 3:
            own_a.wait()
            own_e.wait()
            own_g.wait()
            for d in range(1, NODES):
                a_copy(d, peer(-d)).wait_recv()
            at[...] = abuf[...].reshape(NODES * TOK, SHARD).T
        if t >= 4:
            chunk = t - 4
            for way in range(2):
                g_copy(way, chunk, 3, behind(way, 4)).wait_recv()
            compute(chunk)
    for d in range(1, NODES):
        a_copy(d, me).wait_send()
    for way in range(2):
        for chunk in range(CHUNKS):
            for hop in range(4):
                g_copy(way, chunk, hop, behind(way, hop)).wait_send()


def memory_of(a, g, err):
    anywhere = pl.BlockSpec(memory_space=pl.ANY)
    return pl.pallas_call(
        gather_kernel,
        out_shape=jax.ShapeDtypeStruct((SHARD, D), jnp.float32),
        in_specs=[anywhere] * 3,
        out_specs=pl.BlockSpec(memory_space=pltpu.VMEM),
        scratch_shapes=[
            pltpu.VMEM((NODES, TOK, D), jnp.bfloat16),
            pltpu.VMEM((NODES, TOK, SHARD), jnp.bfloat16),
            pltpu.VMEM((SHARD, NODES * TOK), jnp.bfloat16),
            pltpu.VMEM((SHARD, D), jnp.bfloat16),
            pltpu.SemaphoreType.DMA((NODES,)),
            pltpu.SemaphoreType.DMA((NODES,)),
            pltpu.SemaphoreType.DMA((2, CHUNKS, 4)),
            pltpu.SemaphoreType.DMA((2, CHUNKS, 4)),
            pltpu.SemaphoreType.DMA((3,)),
        ],
        compiler_params=pltpu.CompilerParams(
            collective_id=0, has_side_effects=True, vmem_limit_bytes=48 * 2**20
        ),
        cost_estimate=pl.CostEstimate(flops=2 * 2560 * 256 * 3968 * 20, bytes_accessed=40 * 2**20, transcendentals=0),
        name="gather_grad",
    )(a, g, err)


def back_kernel(g_ref, w_ref, out_ref):
    w = w_ref[...].reshape(SHARD, D)
    out_ref[...] = lax.dot_general(
        g_ref[...], w, (((1,), (1,)), ((), ())), preferred_element_type=jnp.float32
    ).astype(jnp.bfloat16)


def back_of(g, w):
    return pl.pallas_call(
        back_kernel,
        out_shape=jax.ShapeDtypeStruct((TOK, NODES * SHARD), jnp.bfloat16),
        grid=(NODES,),
        in_specs=[
            pl.BlockSpec((TOK, D), lambda n: (0, 0)),
            pl.BlockSpec((32, 1, 8, D), lambda n: (0, n, 0, 0)),
        ],
        out_specs=pl.BlockSpec((TOK, SHARD), lambda n: (0, n)),
        compiler_params=pltpu.CompilerParams(vmem_limit_bytes=32 * 2**20),
        name="input_grad",
    )(g, w)


def shards(attn_out, out_grad, weight, error, q_prev):
    highest = lax.Precision.HIGHEST
    feats = attn_out[0]
    cotan = out_grad[0]
    at = lax.axis_index("rep")
    piece = lax.dynamic_slice(weight, (at * 8, 0), (8, D))
    column = lax.all_gather(piece, "node", axis=0)
    whole = lax.all_gather(column, "rep", axis=0)
    memory = memory_of(feats, cotan, error[0])
    input_grad = back_of(cotan, whole)
    left_local = lax.dot_general(
        q_prev[0],
        memory,
        (((1,), (1,)), ((), ())),
        precision=highest,
        preferred_element_type=jnp.float32,
    )
    left = lax.psum(left_local, "rep")
    gram = jnp.dot(left, left.T, precision=highest)
    lower_factor = jnp.linalg.cholesky(gram)
    basis = jax.scipy.linalg.solve_triangular(lower_factor, left, lower=True)
    right_local = jnp.dot(basis, memory, precision=highest)
    right = lax.psum(right_local, "rep") / lax.axis_size("rep")
    approx = lax.dot_general(
        basis,
        right,
        (((0,), (0,)), ((), ())),
        precision=highest,
        preferred_element_type=jnp.float32,
    )
    new_error = (memory - approx).astype(jnp.bfloat16)
    return (input_grad[None], new_error[None], basis, right[None])


def solution(mesh):
    in_specs = (
        P("rep", "node", None),
        P("rep", "node", None),
        P("node", None),
        P("rep", "node", None),
        P("node", None, None),
    )
    out_specs = (
        P("rep", "node", None),
        P("rep", "node", None),
        P(None, "node"),
        P("node", None, None),
    )
    return jax.shard_map(shards, mesh=mesh, in_specs=in_specs, out_specs=out_specs, check_vma=False)
```

```python
import types

import jax
import jax.numpy as jnp
from jax import lax
from jax.experimental import pallas as pl
from jax.experimental.pallas import tpu as pltpu
from jax.sharding import PartitionSpec as P

MESH = pl.DeviceIdType.MESH
BF16, F32 = jnp.bfloat16, jnp.float32
NODES = 8
SIDE = 4
REPS = 32
TOK = 320
SHARD = 256
RANK = 32
FEATS = NODES * SHARD
D = 3968
WIDE = 4096
WIDTHS = (640, 640, 640, 640, 512, 512, 256, 128)
STARTS = tuple(sum(WIDTHS[:i]) for i in range(len(WIDTHS)))
CHUNKS = len(WIDTHS)
SPLIT = 160

DMA = pltpu.SemaphoreType.DMA
SCRATCH = dict(
    gbuf=pltpu.VMEM((NODES, TOK, D), BF16),
    abuf=pltpu.VMEM((NODES, TOK, SHARD), BF16),
    at=pltpu.VMEM((SHARD, NODES * TOK), BF16),
    avm=pltpu.VMEM((TOK, FEATS), BF16),
    errbuf=pltpu.VMEM((SHARD, D), BF16),
    mem=pltpu.VMEM((SHARD, D), F32),
    wbuf=pltpu.VMEM((NODES, SIDE, SIDE, 16, D), BF16),
    qbuf=pltpu.VMEM((NODES, RANK, WIDE), F32),
    qloc=pltpu.VMEM((RANK, WIDE), F32),
    qsp=pltpu.VMEM((3 * 2 * RANK, D), BF16),
    lbuf=pltpu.VMEM((NODES, RANK, SHARD), F32),
    lrx=pltpu.VMEM((NODES, RANK // 2, SHARD), F32),
    l2=pltpu.VMEM((NODES, RANK // 2, SHARD), F32),
    lz=pltpu.VMEM((NODES, RANK // 2, SHARD), F32),
    lx=pltpu.VMEM((SIDE, RANK // 2, SHARD), F32),
    ly=pltpu.VMEM((SIDE, RANK // 2, SHARD), F32),
    left=pltpu.VMEM((RANK, SHARD), F32),
    basis=pltpu.VMEM((RANK, SHARD), F32),
    b3=pltpu.VMEM((3 * RANK, SHARD), BF16),
    bt6=pltpu.VMEM((SHARD, 6 * RANK), BF16),
    rs=pltpu.VMEM((RANK, D), F32),
    rc=pltpu.VMEM((RANK, D), F32),
    rx=pltpu.VMEM((SIDE, RANK, D), F32),
    ry=pltpu.VMEM((SIDE, RANK, D), F32),
    qo=pltpu.VMEM((RANK, D), F32),
    local=DMA((8,)),
    out=DMA((CHUNKS,)),
    a_s=DMA((NODES,)), a_r=DMA((NODES,)),
    g_s=DMA((2, CHUNKS, 4)), g_r=DMA((2, CHUNKS, 4)),
    qz_s=DMA((4,)), qz_r=DMA((4,)),
    qx_s=DMA((4,)), qx_r=DMA((4,)),
    qy_s=DMA((4,)), qy_r=DMA((4,)),
    qc_s=DMA((1,)), qc_r=DMA((1,)),
    wz_s=DMA((4,)), wz_r=DMA((4,)),
    wx_s=DMA((2, 4)), wx_r=DMA((2, 4)),
    wy_s=DMA((2, 4)), wy_r=DMA((2, 4)),
    wc_s=DMA((4,)), wc_r=DMA((4,)),
    lc_s=DMA((2,)), lc_r=DMA((2,)),
    lz_s=DMA((NODES,)), lz_r=DMA((NODES,)),
    lx_s=DMA((4,)), lx_r=DMA((4,)),
    ly_s=DMA((4,)), ly_r=DMA((4,)),
    rc_s=DMA((CHUNKS,)), rc_r=DMA((CHUNKS,)),
    rx_s=DMA((CHUNKS, 4)), rx_r=DMA((CHUNKS, 4)),
    ry_s=DMA((CHUNKS, 4)), ry_r=DMA((CHUNKS, 4)),
)


def split3(value):
    high = value.astype(BF16)
    rest = value - high.astype(F32)
    middle = rest.astype(BF16)
    low = (rest - middle.astype(F32)).astype(BF16)
    return high, middle, low


def dot_nt(a, b):
    return lax.dot_general(a, b, (((1,), (1,)), ((), ())), preferred_element_type=F32)


def dot_nn(a, b):
    return jnp.dot(a, b, preferred_element_type=F32)


def thirds(value, rows):
    return value[:rows] + value[rows : 2 * rows] + value[2 * rows :]


def fused_kernel(
    a_hbm, g_hbm, w_hbm, e_hbm, q_hbm, ig_hbm, ne_hbm, p_hbm, qo_hbm, *scratch
):
    s = types.SimpleNamespace(**dict(zip(SCRATCH, scratch)))
    me = lax.axis_index("node")
    rep = lax.axis_index("rep")
    x = lax.div(rep, 2 * SIDE)
    y = lax.rem(lax.div(rep, 2), SIDE)
    core = lax.rem(rep, 2)
    chip = y * SIDE + x

    def node(d):
        return lax.rem(me + d + 2 * NODES, NODES)

    def along(v, k):
        return lax.rem(v + k + SIDE, SIDE)

    def z_peer(d):
        return {"node": node(d)}

    def x_peer(k):
        return {"rep": along(x, k) * 2 * SIDE + y * 2 + core}

    def y_peer(k):
        return {"rep": x * 2 * SIDE + along(y, k) * 2 + core}

    twin = {"rep": x * 2 * SIDE + y * 2 + (1 - core)}

    def remote(src, dst, send_sem, recv_sem, device):
        return pltpu.make_async_remote_copy(
            src_ref=src, dst_ref=dst, send_sem=send_sem, recv_sem=recv_sem,
            device_id=device, device_id_type=MESH,
        )

    def plane_of(slot):
        return lax.rem(me + jnp.where(slot < 4, 7 - slot, slot - 4), NODES)

    def part(start, size):
        return pl.ds(pl.multiple_of(start, size), size)

    mine = part(core * 4, 4)
    chip_cols = part(chip * 256, 256)

    barrier = pltpu.get_barrier_semaphore()
    friends = [z_peer(d) for d in range(1, NODES)]
    friends += [x_peer(k) for k in range(1, SIDE)] + [y_peer(k) for k in range(1, SIDE)] + [twin]
    for friend in friends:
        pl.semaphore_signal(barrier, inc=1, device_id=friend, device_id_type=MESH)

    own_q = pltpu.make_async_copy(q_hbm, s.qloc.at[:, pl.ds(0, D)], s.local.at[0])
    own_q.start()
    own_g = pltpu.make_async_copy(g_hbm, s.gbuf.at[me], s.local.at[1])
    own_g.start()
    own_a = pltpu.make_async_copy(a_hbm.at[:, part(me * SHARD, SHARD)], s.abuf.at[me], s.local.at[2])
    own_a.start()
    all_a = pltpu.make_async_copy(a_hbm, s.avm, s.local.at[3])
    all_a.start()
    own_e = pltpu.make_async_copy(e_hbm, s.errbuf, s.local.at[4])
    own_e.start()
    s.qloc[:, D:] = jnp.zeros((RANK, WIDE - D), F32)
    pl.semaphore_wait(barrier, len(friends))
    own_q.wait()

    def qz(i):
        slot = core * 4 + i
        d = jnp.where(core == 0, i + 1, -i)
        return remote(
            s.qloc.at[:, chip_cols], s.qbuf.at[slot, :, chip_cols], s.qz_s.at[i], s.qz_r.at[i], z_peer(d)
        )

    qz_own = pltpu.make_async_copy(s.qloc.at[:, chip_cols], s.qbuf.at[4, :, chip_cols], s.local.at[5])

    def only(which, action):
        pl.when(core == which)(action)

    def qz_start():
        only(0, lambda: qz(0).start())
        only(1, lambda: qz_own.start())
        for i in range(1, 4):
            qz(i).start()

    def qz_wait():
        only(0, lambda: qz(0).wait_recv())
        only(1, lambda: qz_own.wait())
        for i in range(1, 4):
            qz(i).wait_recv()

    def qz_sent():
        only(0, lambda: qz(0).wait_send())
        for i in range(1, 4):
            qz(i).wait_send()

    def qx(k, at):
        region = s.qbuf.at[mine, :, part((y * SIDE + at) * 256, 256)]
        return remote(region, region, s.qx_s.at[k], s.qx_r.at[k], x_peer(k))

    def qy(k, at):
        region = s.qbuf.at[mine, :, part(at * 1024, 1024)]
        return remote(region, region, s.qy_s.at[k], s.qy_r.at[k], y_peer(k))

    def qc(at):
        region = s.qbuf.at[part(at * 4, 4)]
        return remote(region, region, s.qc_s.at[0], s.qc_r.at[0], twin)

    w_rows = w_hbm.at[part(chip * 16, 16)]
    onward = {"node": lax.rem(me + jnp.where(core == 0, 1, NODES - 1), NODES)}

    def wz(i):
        slot = core * 4 + i
        src = w_rows if i == 0 else s.wbuf.at[slot - 1, y, x]
        return remote(src, s.wbuf.at[slot, y, x], s.wz_s.at[i], s.wz_r.at[i], onward)

    wz_own = pltpu.make_async_copy(w_rows, s.wbuf.at[4, y, x], s.local.at[6])

    def wz_start(i):
        if i == 0:
            only(0, lambda: wz(0).start())
            only(1, lambda: wz_own.start())
        else:
            wz(i).start()

    def wz_wait(i):
        if i == 0:
            only(0, lambda: wz(0).wait_recv())
            only(1, lambda: wz_own.wait())
        else:
            wz(i).wait_recv()

    def w_step(half, step, k, at):
        slots = part(core * 4 + 2 * half, 2)
        if (half == 0) == (step == 0):
            if step == 0:
                region = s.wbuf.at[slots, y, at]
            else:
                region = s.wbuf.at[slots, :, at]
            return remote(region, region, s.wx_s.at[half, k], s.wx_r.at[half, k], x_peer(k))
        if step == 0:
            region = s.wbuf.at[slots, at, x]
        else:
            region = s.wbuf.at[slots, at]
        return remote(region, region, s.wy_s.at[half, k], s.wy_r.at[half, k], y_peer(k))

    def w_where(half, step):
        return x if (half == 0) == (step == 0) else y

    def w_start(step):
        for half in range(2):
            for k in range(1, SIDE):
                w_step(half, step, k, w_where(half, step)).start()

    def w_wait(step):
        for half in range(2):
            for k in range(1, SIDE):
                w_step(half, step, k, along(w_where(half, step), -k)).wait_recv()

    def wc(i, at):
        region = s.wbuf.at[at * 4 + i]
        return remote(region, region, s.wc_s.at[i], s.wc_r.at[i], twin)

    def a_copy(d, at):
        to = node(d)
        return remote(a_hbm.at[:, part(to * SHARD, SHARD)], s.abuf.at[at], s.a_s.at[d], s.a_r.at[d], {"node": to})

    def g_copy(way, chunk, hop):
        source = node(-hop if way == 0 else hop)
        if hop < 3:
            rows = pl.ds(0, TOK)
        else:
            rows = pl.ds(0, SPLIT) if way == 0 else pl.ds(SPLIT, TOK - SPLIT)
        cols = pl.ds(STARTS[chunk], WIDTHS[chunk])
        dst = s.gbuf.at[source, rows, cols]
        src = g_hbm.at[:, cols] if hop == 0 else dst
        return remote(
            src, dst, s.g_s.at[way, chunk, hop], s.g_r.at[way, chunk, hop], z_peer(1 if way == 0 else -1)
        )

    def g_arrived(way, chunk, hop):
        source = node(-hop - 1 if way == 0 else hop + 1)
        if hop < 3:
            rows = pl.ds(0, TOK)
        else:
            rows = pl.ds(0, SPLIT) if way == 0 else pl.ds(SPLIT, TOK - SPLIT)
        region = s.gbuf.at[source, rows, pl.ds(STARTS[chunk], WIDTHS[chunk])]
        remote(
            region, region, s.g_s.at[way, chunk, hop], s.g_r.at[way, chunk, hop], z_peer(1 if way == 0 else -1)
        ).wait_recv()

    def left_terms():
        own_g.wait()
        all_a.wait()
        own_e.wait()

        def pair(half, carry):
            for i in range(2):
                pieces = split3(s.qbuf[2 * half + i, :, pl.ds(0, D)])
                for j in range(3):
                    s.qsp[pl.ds(64 * j + 32 * i, RANK), :] = pieces[j]
            pieces = split3(thirds(dot_nt(s.qsp[...], s.gbuf[me]), 2 * RANK))
            for i in range(2):
                plane = plane_of(2 * half + i)
                stacked = jnp.concatenate([piece[RANK * i : RANK * (i + 1)] for piece in pieces], axis=0)
                s.lbuf[plane] = thirds(dot_nn(stacked, s.avm[:, part(plane * SHARD, SHARD)]), RANK)
            return carry

        lax.fori_loop(0, 4, pair, 0)
        pieces = split3(s.qloc[:, pl.ds(0, D)])
        s.lbuf[me] += thirds(dot_nt(jnp.concatenate(pieces, axis=0), s.errbuf[...]), RANK)

    def lc0(at):
        return remote(
            s.lbuf.at[:, part((1 - at) * 16, 16)], s.lrx, s.lc_s.at[0], s.lc_r.at[0], twin
        )

    def lzc(d, at):
        to = node(d)
        return remote(s.l2.at[to], s.lz.at[at], s.lz_s.at[d], s.lz_r.at[d], {"node": to})

    def lxc(k, at):
        return remote(s.lx.at[at], s.lx.at[at], s.lx_s.at[k], s.lx_r.at[k], x_peer(k))

    def lyc(k, at):
        return remote(s.ly.at[at], s.ly.at[at], s.ly_s.at[k], s.ly_r.at[k], y_peer(k))

    def lc1(at):
        region = s.left.at[part(at * 16, 16)]
        return remote(region, region, s.lc_s.at[1], s.lc_r.at[1], twin)

    def left_0():
        left_terms()
        lc0(core).start()

    def left_1():
        lc0(core).wait_recv()
        s.l2[...] = s.lbuf[:, part(core * 16, 16), :] + s.lrx[...]
        for d in range(1, NODES):
            lzc(d, me).start()
        s.lz[me] = s.l2[me]

    def added(ref, count):
        total = ref[0]
        for i in range(1, count):
            total = total + ref[i]
        return total

    def left_2():
        for d in range(1, NODES):
            lzc(d, node(-d)).wait_recv()
        s.lx[x] = added(s.lz, NODES)
        for k in range(1, SIDE):
            lxc(k, x).start()

    def left_3():
        for k in range(1, SIDE):
            lxc(k, along(x, -k)).wait_recv()
        s.ly[y] = added(s.lx, SIDE)
        for k in range(1, SIDE):
            lyc(k, y).start()

    def left_4():
        for k in range(1, SIDE):
            lyc(k, along(y, -k)).wait_recv()
        s.left[part(core * 16, 16), :] = added(s.ly, SIDE)
        lc1(core).start()

    def left_5():
        lc1(1 - core).wait_recv()
        left = s.left[...]
        gram = lax.dot_general(
            left, left, (((1,), (1,)), ((), ())), precision=lax.Precision.HIGHEST, preferred_element_type=F32
        )
        row_g = lax.broadcasted_iota(jnp.int32, (RANK, RANK), 0)
        col_g = lax.broadcasted_iota(jnp.int32, (RANK, RANK), 1)
        row_l = lax.broadcasted_iota(jnp.int32, (RANK, SHARD), 0)
        row_1 = lax.broadcasted_iota(jnp.int32, (RANK, 1), 0)

        def step(k, carry):
            gram, left = carry
            column = jnp.sum(jnp.where(col_g == k, gram, 0.0), axis=1, keepdims=True)
            pivot = jnp.sum(jnp.where(row_1 == k, column, 0.0), axis=0, keepdims=True)
            scale = 1.0 / jnp.sqrt(pivot)
            top_g = jnp.sum(jnp.where(row_g == k, gram, 0.0), axis=0, keepdims=True) * scale
            top_l = jnp.sum(jnp.where(row_l == k, left, 0.0), axis=0, keepdims=True) * scale
            below = jnp.where(row_1 > k, column * scale, 0.0)
            gram = jnp.where(row_g == k, top_g, gram - below * top_g)
            left = jnp.where(row_l == k, top_l, left - below * top_l)
            return gram, left

        _, basis = lax.fori_loop(0, RANK, step, (gram, left))
        s.basis[...] = basis
        high, middle, low = split3(basis)
        s.b3[...] = jnp.concatenate([high, middle, low], axis=0)
        s.bt6[...] = jnp.concatenate([basis, basis, middle.astype(F32), middle.astype(F32), high.astype(F32), low.astype(F32)], axis=0).T.astype(BF16)

    p_copy = pltpu.make_async_copy(s.basis, p_hbm, s.local.at[7])

    def cols_of(chunk):
        return pl.ds(STARTS[chunk], WIDTHS[chunk])

    def start_memory():
        own_a.wait()
        for d in range(1, NODES):
            a_copy(d, node(-d)).wait_recv()
        s.at[...] = s.abuf[...].reshape(NODES * TOK, SHARD).T

    def memory_of(chunk):
        cols = cols_of(chunk)
        block = s.gbuf[:, :, cols].reshape(NODES * TOK, WIDTHS[chunk])
        s.mem[:, cols] = dot_nn(s.at[...], block) + s.errbuf[:, cols].astype(F32)

    def rcc(chunk):
        cols = cols_of(chunk)
        return remote(s.rs.at[:, cols], s.rc.at[:, cols], s.rc_s.at[chunk], s.rc_r.at[chunk], twin)

    def rxc(chunk, k, at):
        region = s.rx.at[at, :, cols_of(chunk)]
        return remote(region, region, s.rx_s.at[chunk, k], s.rx_r.at[chunk, k], x_peer(k))

    def ryc(chunk, k, at):
        region = s.ry.at[at, :, cols_of(chunk)]
        return remote(region, region, s.ry_s.at[chunk, k], s.ry_r.at[chunk, k], y_peer(k))

    def right_0(chunk):
        cols = cols_of(chunk)
        high, middle, low = split3(s.mem[:, cols])
        total = thirds(dot_nn(s.b3[...], high), RANK)
        second = dot_nn(s.b3[: 2 * RANK], middle)
        s.rs[:, cols] = total + (second[:RANK] + second[RANK:]) + dot_nn(s.b3[:RANK], low)
        rcc(chunk).start()

    def right_1(chunk):
        cols = cols_of(chunk)
        rcc(chunk).wait_recv()
        s.rx[x, :, cols] = s.rs[:, cols] + s.rc[:, cols]
        for k in range(1, SIDE):
            rxc(chunk, k, x).start()

    def right_2(chunk):
        cols = cols_of(chunk)
        for k in range(1, SIDE):
            rxc(chunk, k, along(x, -k)).wait_recv()
        s.ry[y, :, cols] = ((s.rx[0, :, cols] + s.rx[1, :, cols]) + s.rx[2, :, cols]) + s.rx[3, :, cols]
        for k in range(1, SIDE):
            ryc(chunk, k, y).start()

    def ne_copy(chunk):
        cols = cols_of(chunk)
        return pltpu.make_async_copy(s.errbuf.at[:, cols], ne_hbm.at[:, cols], s.out.at[chunk])

    def right_3(chunk):
        cols = cols_of(chunk)
        for k in range(1, SIDE):
            ryc(chunk, k, along(y, -k)).wait_recv()
        total = ((s.ry[0, :, cols] + s.ry[1, :, cols]) + s.ry[2, :, cols]) + s.ry[3, :, cols]
        right = total * (1.0 / REPS)
        s.qo[:, cols] = right
        high, middle, low = split3(right)
        approx = dot_nn(s.bt6[...], jnp.concatenate([high, middle, high, middle, low, high], axis=0))
        s.errbuf[:, cols] = (s.mem[:, cols] - approx).astype(BF16)
        ne_copy(chunk).start()

    def back(slot):
        plane = plane_of(slot)
        block = s.wbuf[slot].reshape(SHARD, D)
        s.avm[:, part(plane * SHARD, SHARD)] = dot_nt(s.gbuf[me], block).astype(BF16)

    def back_own(i):
        back(core * 4 + i)

    def back_twin(i):
        wc(i, 1 - core).wait_recv()
        back((1 - core) * 4 + i)

    ig_copy = pltpu.make_async_copy(s.avm, ig_hbm, s.local.at[3])

    def q_over_x():
        qz_wait()
        for k in range(1, SIDE):
            qx(k, x).start()

    def q_over_y():
        for k in range(1, SIDE):
            qx(k, along(x, -k)).wait_recv()
        for k in range(1, SIDE):
            qy(k, y).start()

    def q_over_cores():
        for k in range(1, SIDE):
            qy(k, along(y, -k)).wait_recv()
        qc(core).start()

    def q_done():
        qc(1 - core).wait_recv()

    def w_hop(i):
        wz_wait(i - 1)
        if i < 4:
            wz_start(i)
        else:
            w_start(0)

    def w_middle():
        w_wait(0)
        w_start(1)

    def w_cores():
        w_wait(1)
        for i in range(4):
            wc(i, core).start()

    tasks = {
        (0, 3): [q_over_x, lambda: w_hop(1), q_over_y, lambda: w_hop(2)],
        (1, 3): [lambda: w_hop(3), q_over_cores],
        (2, 2): [lambda: w_hop(4)],
        (2, 3): [q_done, left_0],
        (3, 1): [left_1],
        (3, 3): [w_middle, left_2],
        (4, 1): [left_3],
        (4, 2): [left_4],
        (4, 3): [left_5],
        (5, 2): [w_cores],
        (6, 1): [lambda: back_own(0), lambda: back_own(1)],
        (6, 2): [lambda: back_own(2), lambda: back_own(3)],
        (7, 1): [lambda: back_twin(0), lambda: back_twin(1)],
        (7, 2): [lambda: back_twin(2), lambda: back_twin(3), ig_copy.start],
    }
    stages = [memory_of, right_0, right_1, right_2, right_3]

    qz_start()
    wz_start(0)
    for d in (4, 3, 5, 2, 6, 1, 7):
        a_copy(d, me).start()
    ready = 5
    queue = []
    for t in range(CHUNKS + 4):
        for hop in range(4):
            chunk = t - hop
            if 0 <= chunk < CHUNKS:
                for way in range(2):
                    if hop:
                        g_arrived(way, chunk, hop - 1)
                    g_copy(way, chunk, hop).start()
            for task in tasks.get((t, hop), ()):
                task()
            if hop < 3 and t >= ready and queue:
                queue = [(c, n + 1) for c, n in queue if stages[n](c) is None and n < 4]
        if t == 3:
            start_memory()
        if t >= 4:
            for way in range(2):
                g_arrived(way, t - 4, 3)
            memory_of(t - 4)
            queue.append((t - 4, 1))
    while queue:
        queue = [(c, n + 1) for c, n in queue if stages[n](c) is None and n < 4]

    p_copy.start()
    q_copy = pltpu.make_async_copy(s.qo, qo_hbm, s.local.at[0])
    q_copy.start()
    qz_sent()
    only(0, lambda: wz(0).wait_send())
    for i in range(1, 4):
        wz(i).wait_send()
    for k in range(1, SIDE):
        qx(k, x).wait_send()
        qy(k, y).wait_send()
        lxc(k, x).wait_send()
        lyc(k, y).wait_send()
        for half in range(2):
            for step in range(2):
                w_step(half, step, k, w_where(half, step)).wait_send()
        for chunk in range(CHUNKS):
            rxc(chunk, k, x).wait_send()
            ryc(chunk, k, y).wait_send()
    qc(core).wait_send()
    lc0(core).wait_send()
    lc1(core).wait_send()
    for i in range(4):
        wc(i, core).wait_send()
    for d in range(1, NODES):
        a_copy(d, me).wait_send()
        lzc(d, me).wait_send()
    for chunk in range(CHUNKS):
        rcc(chunk).wait_send()
        for way in range(2):
            for hop in range(4):
                g_copy(way, chunk, hop).wait_send()
        ne_copy(chunk).wait()
    ig_copy.wait()
    p_copy.wait()
    q_copy.wait()


def shards(attn_out, out_grad, weight, error, q_prev):
    anywhere = pl.BlockSpec(memory_space=pl.ANY)
    input_grad, new_error, p_out, q_out = pl.pallas_call(
        fused_kernel,
        out_shape=(
            jax.ShapeDtypeStruct((TOK, FEATS), BF16),
            jax.ShapeDtypeStruct((SHARD, D), BF16),
            jax.ShapeDtypeStruct((RANK, SHARD), F32),
            jax.ShapeDtypeStruct((RANK, D), F32),
        ),
        in_specs=[anywhere] * 5,
        out_specs=[anywhere] * 4,
        scratch_shapes=list(SCRATCH.values()),
        compiler_params=pltpu.CompilerParams(
            collective_id=0, has_side_effects=True, vmem_limit_bytes=63 * 2**20
        ),
        name="powersgd",
    )(attn_out[0], out_grad[0], weight, error[0], q_prev[0])
    return input_grad[None], new_error[None], p_out, q_out[None]


def solution(mesh):
    in_specs = (
        P("rep", "node", None),
        P("rep", "node", None),
        P("node", None),
        P("rep", "node", None),
        P("node", None, None),
    )
    out_specs = (
        P("rep", "node", None),
        P("rep", "node", None),
        P(None, "node"),
        P("node", None, None),
    )
    return jax.shard_map(shards, mesh=mesh, in_specs=in_specs, out_specs=out_specs, check_vma=False)
```

```python
import types

import jax
import jax.numpy as jnp
from jax import lax
from jax.experimental import pallas as pl
from jax.experimental.pallas import tpu as pltpu
from jax.sharding import PartitionSpec as P

MESH = pl.DeviceIdType.MESH
BF16, F32 = jnp.bfloat16, jnp.float32
NODES = 8
SIDE = 4
REPS = 32
TOK = 320
SHARD = 256
RANK = 32
FEATS = NODES * SHARD
D = 3968
WIDE = 4096
WIDTHS = (768, 768, 640, 640, 512, 384, 128, 128)
STARTS = tuple(sum(WIDTHS[:i]) for i in range(len(WIDTHS)))
CHUNKS = len(WIDTHS)
FAST = 6
FAST_AT = STARTS[FAST]
CALM = CHUNKS - 1
AHEAD = 1
SPLIT = 160

DMA = pltpu.SemaphoreType.DMA
SCRATCH = dict(
    gbuf=pltpu.VMEM((NODES, TOK, D), BF16),
    abuf=pltpu.VMEM((NODES, TOK, SHARD), BF16),
    at=pltpu.VMEM((SHARD, NODES * TOK), BF16),
    avm=pltpu.VMEM((TOK, FEATS), BF16),
    errbuf=pltpu.VMEM((SHARD, D), BF16),
    mem=pltpu.VMEM((SHARD, D), F32),
    wbuf=pltpu.VMEM((NODES, SIDE, SIDE, 16, D), BF16),
    qbuf=pltpu.VMEM((NODES, RANK, WIDE), F32),
    qloc=pltpu.VMEM((RANK, WIDE), F32),
    qsp=pltpu.VMEM((3 * 2 * RANK, D), BF16),
    lbuf=pltpu.VMEM((NODES, RANK, SHARD), F32),
    lrx=pltpu.VMEM((NODES, RANK // 2, SHARD), F32),
    l2=pltpu.VMEM((NODES, RANK // 2, SHARD), F32),
    lz=pltpu.VMEM((NODES, RANK // 2, SHARD), F32),
    lx=pltpu.VMEM((SIDE, RANK // 2, SHARD), F32),
    ly=pltpu.VMEM((SIDE, RANK // 2, SHARD), F32),
    left=pltpu.VMEM((RANK, SHARD), F32),
    basis=pltpu.VMEM((RANK, SHARD), F32),
    b3=pltpu.VMEM((3 * RANK, SHARD), BF16),
    bt6=pltpu.VMEM((SHARD, 6 * RANK), BF16),
    rs=pltpu.VMEM((RANK, D), F32),
    rc=pltpu.VMEM((RANK // 2, D), F32),
    rx=pltpu.VMEM((SIDE, RANK // 2, D), F32),
    ry=pltpu.VMEM((SIDE, RANK // 2, D), F32),
    qo=pltpu.VMEM((RANK, D), F32),
    rf=pltpu.VMEM((2 * SIDE, RANK, D - FAST_AT), F32),
    rg=pltpu.VMEM((SIDE, RANK, D - FAST_AT), F32),
    local=DMA((8,)),
    out=DMA((CHUNKS,)),
    a_s=DMA((NODES,)), a_r=DMA((NODES,)),
    g_s=DMA((2, CHUNKS, 4)), g_r=DMA((2, CHUNKS, 4)),
    qz_s=DMA((4,)), qz_r=DMA((4,)),
    qx_s=DMA((4,)), qx_r=DMA((4,)),
    qy_s=DMA((4,)), qy_r=DMA((4,)),
    qc_s=DMA((1,)), qc_r=DMA((1,)),
    wz_s=DMA((4,)), wz_r=DMA((4,)),
    wx_s=DMA((2, 4)), wx_r=DMA((2, 4)),
    wy_s=DMA((2, 4)), wy_r=DMA((2, 4)),
    wc_s=DMA((4,)), wc_r=DMA((4,)),
    lc_s=DMA((2,)), lc_r=DMA((2,)),
    lz_s=DMA((NODES,)), lz_r=DMA((NODES,)),
    lx_s=DMA((4,)), lx_r=DMA((4,)),
    ly_s=DMA((4,)), ly_r=DMA((4,)),
    rc_s=DMA((CHUNKS,)), rc_r=DMA((CHUNKS,)),
    rd_s=DMA((CHUNKS,)), rd_r=DMA((CHUNKS,)),
    rf_s=DMA((CHUNKS, 8)), rf_r=DMA((CHUNKS, 8)),
    rx_s=DMA((CHUNKS, 4)), rx_r=DMA((CHUNKS, 4)),
    ry_s=DMA((CHUNKS, 4)), ry_r=DMA((CHUNKS, 4)),
)


def split3(value):
    high = value.astype(BF16)
    rest = value - high.astype(F32)
    middle = rest.astype(BF16)
    low = (rest - middle.astype(F32)).astype(BF16)
    return high, middle, low


def dot_nt(a, b):
    return lax.dot_general(a, b, (((1,), (1,)), ((), ())), preferred_element_type=F32)


def dot_nn(a, b):
    return jnp.dot(a, b, preferred_element_type=F32)


def thirds(value, rows):
    return value[:rows] + value[rows : 2 * rows] + value[2 * rows :]


def fused_kernel(
    a_hbm, g_hbm, w_hbm, e_hbm, q_hbm, ig_hbm, ne_hbm, p_hbm, qo_hbm, *scratch
):
    s = types.SimpleNamespace(**dict(zip(SCRATCH, scratch)))
    me = lax.axis_index("node")
    rep = lax.axis_index("rep")
    x = lax.div(rep, 2 * SIDE)
    y = lax.rem(lax.div(rep, 2), SIDE)
    core = lax.rem(rep, 2)
    chip = y * SIDE + x

    def node(d):
        return lax.rem(me + d + 2 * NODES, NODES)

    def along(v, k):
        return lax.rem(v + k + SIDE, SIDE)

    def z_peer(d):
        return {"node": node(d)}

    def x_peer(k):
        return {"rep": along(x, k) * 2 * SIDE + y * 2 + core}

    def y_peer(k):
        return {"rep": x * 2 * SIDE + along(y, k) * 2 + core}

    def pair_peer(k):
        other = lax.rem(x * 2 + core + k, 2 * SIDE)
        return {"rep": lax.div(other, 2) * 2 * SIDE + y * 2 + lax.rem(other, 2)}

    twin = {"rep": x * 2 * SIDE + y * 2 + (1 - core)}

    def remote(src, dst, send_sem, recv_sem, device):
        return pltpu.make_async_remote_copy(
            src_ref=src, dst_ref=dst, send_sem=send_sem, recv_sem=recv_sem,
            device_id=device, device_id_type=MESH,
        )

    def plane_of(slot):
        return lax.rem(me + (jnp.where(slot < 4, 7 - slot, slot - 4)), NODES)

    def part(start, size):
        return pl.ds(pl.multiple_of(start, size), size)

    mine = part(core * 4, 4)
    chip_cols = part(chip * 256, 256)

    barrier = pltpu.get_barrier_semaphore()
    friends = [z_peer(d) for d in range(1, NODES)]
    friends += [pair_peer(k) for k in range(1, 2 * SIDE)] + [y_peer(k) for k in range(1, SIDE)]
    for friend in friends:
        pl.semaphore_signal(barrier, inc=1, device_id=friend, device_id_type=MESH)

    own_q = pltpu.make_async_copy(q_hbm, s.qloc.at[:, pl.ds(0, D)], s.local.at[0])
    own_q.start()
    own_g = pltpu.make_async_copy(g_hbm, s.gbuf.at[me], s.local.at[1])
    own_g.start()
    own_a = pltpu.make_async_copy(a_hbm.at[:, part(me * SHARD, SHARD)], s.abuf.at[me], s.local.at[2])
    own_a.start()
    all_a = pltpu.make_async_copy(a_hbm, s.avm, s.local.at[3])
    all_a.start()
    own_e = pltpu.make_async_copy(e_hbm, s.errbuf, s.local.at[4])
    own_e.start()
    s.qloc[:, D:] = jnp.zeros((RANK, WIDE - D), F32)
    pl.semaphore_wait(barrier, len(friends))
    own_q.wait()

    def qz(i):
        slot = core * 4 + i
        d = jnp.where(core == 0, i + 1, -i)
        return remote(
            s.qloc.at[:, chip_cols], s.qbuf.at[slot, :, chip_cols], s.qz_s.at[i], s.qz_r.at[i], z_peer(d)
        )

    qz_own = pltpu.make_async_copy(s.qloc.at[:, chip_cols], s.qbuf.at[4, :, chip_cols], s.local.at[5])

    def only(which, action):
        pl.when(core == which)(action)

    def qz_start():
        only(0, lambda: qz(0).start())
        only(1, lambda: qz_own.start())
        for i in range(1, 4):
            qz(i).start()

    def qz_wait():
        only(0, lambda: qz(0).wait_recv())
        only(1, lambda: qz_own.wait())
        for i in range(1, 4):
            qz(i).wait_recv()

    def qz_sent():
        only(0, lambda: qz(0).wait_send())
        for i in range(1, 4):
            qz(i).wait_send()

    def qx(k, at):
        region = s.qbuf.at[mine, :, part((y * SIDE + at) * 256, 256)]
        return remote(region, region, s.qx_s.at[k], s.qx_r.at[k], x_peer(k))

    def qy(k, at):
        region = s.qbuf.at[mine, :, part(at * 1024, 1024)]
        return remote(region, region, s.qy_s.at[k], s.qy_r.at[k], y_peer(k))

    def qc(at):
        region = s.qbuf.at[part(at * 4, 4)]
        return remote(region, region, s.qc_s.at[0], s.qc_r.at[0], twin)

    w_rows = w_hbm.at[part(chip * 16, 16)]
    onward = {"node": lax.rem(me + jnp.where(core == 0, 1, NODES - 1), NODES)}

    def wz(i):
        slot = core * 4 + i
        src = w_rows if i == 0 else s.wbuf.at[slot - 1, y, x]
        return remote(src, s.wbuf.at[slot, y, x], s.wz_s.at[i], s.wz_r.at[i], onward)

    wz_own = pltpu.make_async_copy(w_rows, s.wbuf.at[4, y, x], s.local.at[6])

    def wz_start(i):
        if i == 0:
            only(0, lambda: wz(0).start())
            only(1, lambda: wz_own.start())
        else:
            wz(i).start()

    def wz_wait(i):
        if i == 0:
            only(0, lambda: wz(0).wait_recv())
            only(1, lambda: wz_own.wait())
        else:
            wz(i).wait_recv()

    def w_step(half, step, k, at):
        slots = part(core * 4 + 2 * half, 2)
        if (half == 0) == (step == 0):
            if step == 0:
                region = s.wbuf.at[slots, y, at]
            else:
                region = s.wbuf.at[slots, :, at]
            return remote(region, region, s.wx_s.at[half, k], s.wx_r.at[half, k], x_peer(k))
        if step == 0:
            region = s.wbuf.at[slots, at, x]
        else:
            region = s.wbuf.at[slots, at]
        return remote(region, region, s.wy_s.at[half, k], s.wy_r.at[half, k], y_peer(k))

    def w_where(half, step):
        return x if (half == 0) == (step == 0) else y

    def w_start(step):
        for half in range(2):
            for k in range(1, SIDE):
                w_step(half, step, k, w_where(half, step)).start()

    def w_wait(step):
        for half in range(2):
            for k in range(1, SIDE):
                w_step(half, step, k, along(w_where(half, step), -k)).wait_recv()

    def wc(i, at):
        region = s.wbuf.at[at * 4 + i]
        return remote(region, region, s.wc_s.at[i], s.wc_r.at[i], twin)

    def a_copy(d, at):
        to = node(d)
        return remote(a_hbm.at[:, part(to * SHARD, SHARD)], s.abuf.at[at], s.a_s.at[d], s.a_r.at[d], {"node": to})

    def g_copy(way, chunk, hop):
        source = node(-hop if way == 0 else hop)
        if hop < 3:
            rows = pl.ds(0, TOK)
        else:
            rows = pl.ds(0, SPLIT) if way == 0 else pl.ds(SPLIT, TOK - SPLIT)
        cols = pl.ds(STARTS[chunk], WIDTHS[chunk])
        dst = s.gbuf.at[source, rows, cols]
        src = g_hbm.at[:, cols] if hop == 0 else dst
        return remote(
            src, dst, s.g_s.at[way, chunk, hop], s.g_r.at[way, chunk, hop], z_peer(1 if way == 0 else -1)
        )

    def g_arrived(way, chunk, hop):
        source = node(-hop - 1 if way == 0 else hop + 1)
        if hop < 3:
            rows = pl.ds(0, TOK)
        else:
            rows = pl.ds(0, SPLIT) if way == 0 else pl.ds(SPLIT, TOK - SPLIT)
        region = s.gbuf.at[source, rows, pl.ds(STARTS[chunk], WIDTHS[chunk])]
        remote(
            region, region, s.g_s.at[way, chunk, hop], s.g_r.at[way, chunk, hop], z_peer(1 if way == 0 else -1)
        ).wait_recv()

    def inputs_here():
        own_g.wait()
        all_a.wait()
        own_e.wait()

    def left_pair(half):
        for i in range(2):
            pieces = split3(s.qbuf[2 * half + i, :, pl.ds(0, D)])
            for j in range(3):
                s.qsp[pl.ds(64 * j + 32 * i, RANK), :] = pieces[j]
        pieces = split3(thirds(dot_nt(s.qsp[...], s.gbuf[me]), 2 * RANK))
        for i in range(2):
            plane = plane_of(2 * half + i)
            stacked = jnp.concatenate([piece[RANK * i : RANK * (i + 1)] for piece in pieces], axis=0)
            s.lbuf[plane] = thirds(dot_nn(stacked, s.avm[:, part(plane * SHARD, SHARD)]), RANK)

    def left_own():
        pieces = split3(s.qloc[:, pl.ds(0, D)])
        s.lbuf[me] += thirds(dot_nt(jnp.concatenate(pieces, axis=0), s.errbuf[...]), RANK)
        lc0(core).start()

    def lc0(at):
        return remote(
            s.lbuf.at[:, part((1 - at) * 16, 16)], s.lrx, s.lc_s.at[0], s.lc_r.at[0], twin
        )

    def lzc(d, at):
        to = node(d)
        return remote(s.l2.at[to], s.lz.at[at], s.lz_s.at[d], s.lz_r.at[d], {"node": to})

    def lxc(k, at):
        return remote(s.lx.at[at], s.lx.at[at], s.lx_s.at[k], s.lx_r.at[k], x_peer(k))

    def lyc(k, at):
        return remote(s.ly.at[at], s.ly.at[at], s.ly_s.at[k], s.ly_r.at[k], y_peer(k))

    def lc1(at):
        region = s.left.at[part(at * 16, 16)]
        return remote(region, region, s.lc_s.at[1], s.lc_r.at[1], twin)

    def left_1():
        lc0(core).wait_recv()
        s.l2[...] = s.lbuf[:, part(core * 16, 16), :] + s.lrx[...]
        for d in range(1, NODES):
            lzc(d, me).start()
        s.lz[me] = s.l2[me]

    def added(ref, count):
        total = ref[0]
        for i in range(1, count):
            total = total + ref[i]
        return total

    def left_2():
        for d in range(1, NODES):
            lzc(d, node(-d)).wait_recv()
        s.lx[x] = added(s.lz, NODES)
        for k in range(1, SIDE):
            lxc(k, x).start()

    def left_3():
        for k in range(1, SIDE):
            lxc(k, along(x, -k)).wait_recv()
        s.ly[y] = added(s.lx, SIDE)
        for k in range(1, SIDE):
            lyc(k, y).start()

    def left_4():
        for k in range(1, SIDE):
            lyc(k, along(y, -k)).wait_recv()
        s.left[part(core * 16, 16), :] = added(s.ly, SIDE)
        lc1(core).start()

    def left_5():
        lc1(1 - core).wait_recv()
        left = s.left[...]
        gram = lax.dot_general(
            left, left, (((1,), (1,)), ((), ())), precision=lax.Precision.HIGHEST, preferred_element_type=F32
        )
        row_g = lax.broadcasted_iota(jnp.int32, (RANK, RANK), 0)
        col_g = lax.broadcasted_iota(jnp.int32, (RANK, RANK), 1)
        row_l = lax.broadcasted_iota(jnp.int32, (RANK, SHARD), 0)
        row_1 = lax.broadcasted_iota(jnp.int32, (RANK, 1), 0)

        def step(k, carry):
            gram, left = carry
            column = jnp.sum(jnp.where(col_g == k, gram, 0.0), axis=1, keepdims=True)
            pivot = jnp.sum(jnp.where(row_1 == k, column, 0.0), axis=0, keepdims=True)
            scale = 1.0 / jnp.sqrt(pivot)
            top_g = jnp.sum(jnp.where(row_g == k, gram, 0.0), axis=0, keepdims=True) * scale
            top_l = jnp.sum(jnp.where(row_l == k, left, 0.0), axis=0, keepdims=True) * scale
            below = jnp.where(row_1 > k, column * scale, 0.0)
            gram = jnp.where(row_g == k, top_g, gram - below * top_g)
            left = jnp.where(row_l == k, top_l, left - below * top_l)
            return gram, left

        _, basis = lax.fori_loop(0, RANK, step, (gram, left))
        s.basis[...] = basis
        high, middle, low = split3(basis)
        s.b3[...] = jnp.concatenate([high, middle, low], axis=0)
        s.bt6[...] = jnp.concatenate([basis, basis, middle.astype(F32), middle.astype(F32), high.astype(F32), low.astype(F32)], axis=0).T.astype(BF16)

    p_copy = pltpu.make_async_copy(s.basis, p_hbm, s.local.at[7])

    def cols_of(chunk):
        return pl.ds(STARTS[chunk], WIDTHS[chunk])

    def start_memory():
        own_a.wait()
        for d in range(1, NODES):
            a_copy(d, node(-d)).wait_recv()
        s.at[...] = s.abuf[...].reshape(NODES * TOK, SHARD).T

    def memory_of(chunk):
        cols = cols_of(chunk)
        block = s.gbuf[:, :, cols].reshape(NODES * TOK, WIDTHS[chunk])
        s.mem[:, cols] = dot_nn(s.at[...], block) + s.errbuf[:, cols].astype(F32)

    def rcc(chunk):
        cols = cols_of(chunk)
        other = part((1 - core) * 16, 16)
        return remote(s.rs.at[other, cols], s.rc.at[:, cols], s.rc_s.at[chunk], s.rc_r.at[chunk], twin)

    def rdc(chunk, at):
        region = s.qo.at[part(at * 16, 16), cols_of(chunk)]
        return remote(region, region, s.rd_s.at[chunk], s.rd_r.at[chunk], twin)

    def rxc(chunk, k, at):
        region = s.rx.at[at, :, cols_of(chunk)]
        return remote(region, region, s.rx_s.at[chunk, k], s.rx_r.at[chunk, k], x_peer(k))

    def ryc(chunk, k, at):
        region = s.ry.at[at, :, cols_of(chunk)]
        return remote(region, region, s.ry_s.at[chunk, k], s.ry_r.at[chunk, k], y_peer(k))

    def right_local(chunk):
        cols = cols_of(chunk)
        high, middle, low = split3(s.mem[:, cols])
        total = thirds(dot_nn(s.b3[...], high), RANK)
        second = dot_nn(s.b3[: 2 * RANK], middle)
        return total + (second[:RANK] + second[RANK:]) + dot_nn(s.b3[:RANK], low)

    def right_0(chunk):
        s.rs[:, cols_of(chunk)] = right_local(chunk)
        rcc(chunk).start()

    def right_1(chunk):
        cols = cols_of(chunk)
        rcc(chunk).wait_recv()
        s.rx[x, :, cols] = s.rs[part(core * 16, 16), cols] + s.rc[:, cols]
        for k in range(1, SIDE):
            rxc(chunk, k, x).start()

    def right_2(chunk):
        cols = cols_of(chunk)
        for k in range(1, SIDE):
            rxc(chunk, k, along(x, -k)).wait_recv()
        s.ry[y, :, cols] = ((s.rx[0, :, cols] + s.rx[1, :, cols]) + s.rx[2, :, cols]) + s.rx[3, :, cols]
        for k in range(1, SIDE):
            ryc(chunk, k, y).start()

    def ne_copy(chunk):
        cols = cols_of(chunk)
        return pltpu.make_async_copy(s.errbuf.at[:, cols], ne_hbm.at[:, cols], s.out.at[chunk])

    def right_3(chunk):
        cols = cols_of(chunk)
        for k in range(1, SIDE):
            ryc(chunk, k, along(y, -k)).wait_recv()
        total = ((s.ry[0, :, cols] + s.ry[1, :, cols]) + s.ry[2, :, cols]) + s.ry[3, :, cols]
        s.qo[part(core * 16, 16), cols] = total * (1.0 / REPS)
        rdc(chunk, core).start()

    def right_4(chunk):
        cols = cols_of(chunk)
        rdc(chunk, 1 - core).wait_recv()
        finish(chunk, s.qo[:, cols])

    def finish(chunk, right):
        cols = cols_of(chunk)
        high, middle, low = split3(right)
        approx = dot_nn(s.bt6[...], jnp.concatenate([high, middle, high, middle, low, high], axis=0))
        s.errbuf[:, cols] = (s.mem[:, cols] - approx).astype(BF16)
        ne_copy(chunk).start()

    def short(chunk):
        return pl.ds(STARTS[chunk] - FAST_AT, WIDTHS[chunk])

    place = x * 2 + core

    def rfc(chunk, k, at):
        region = s.rf.at[at, :, short(chunk)]
        return remote(region, region, s.rf_s.at[chunk, k], s.rf_r.at[chunk, k], pair_peer(k))

    def rgc(chunk, k, at):
        region = s.rg.at[at, :, short(chunk)]
        return remote(region, region, s.ry_s.at[chunk, k], s.ry_r.at[chunk, k], y_peer(k))

    def fast_0(chunk):
        s.rf[place, :, short(chunk)] = right_local(chunk)
        for k in range(1, 2 * SIDE):
            rfc(chunk, k, place).start()

    def fast_1(chunk):
        for k in range(1, 2 * SIDE):
            rfc(chunk, k, lax.rem(place + 2 * SIDE - k, 2 * SIDE)).wait_recv()
        total = s.rf[0, :, short(chunk)]
        for i in range(1, 2 * SIDE):
            total = total + s.rf[i, :, short(chunk)]
        s.rg[y, :, short(chunk)] = total
        for k in range(1, SIDE):
            rgc(chunk, k, y).start()

    def fast_2(chunk):
        for k in range(1, SIDE):
            rgc(chunk, k, along(y, -k)).wait_recv()
        total = s.rg[0, :, short(chunk)]
        for i in range(1, SIDE):
            total = total + s.rg[i, :, short(chunk)]
        right = total * (1.0 / REPS)
        s.qo[:, cols_of(chunk)] = right
        finish(chunk, right)

    def back(slot):
        plane = plane_of(slot)
        block = s.wbuf[slot].reshape(SHARD, D)
        s.avm[:, part(plane * SHARD, SHARD)] = dot_nt(s.gbuf[me], block).astype(BF16)

    def back_own(i):
        back(core * 4 + i)

    def back_twin(i):
        wc(i, 1 - core).wait_recv()
        back((1 - core) * 4 + i)

    ig_copy = pltpu.make_async_copy(s.avm, ig_hbm, s.local.at[3])

    def q_over_x():
        qz_wait()
        for k in range(1, SIDE):
            qx(k, x).start()

    def q_over_y():
        for k in range(1, SIDE):
            qx(k, along(x, -k)).wait_recv()
        for k in range(1, SIDE):
            qy(k, y).start()

    def q_over_cores():
        for k in range(1, SIDE):
            qy(k, along(y, -k)).wait_recv()
        qc(core).start()

    def q_done():
        qc(1 - core).wait_recv()

    def w_hop(i):
        wz_wait(i - 1)
        if i < 4:
            wz_start(i)
        else:
            w_start(0)

    def w_middle():
        w_wait(0)
        w_start(1)

    def w_cores():
        w_wait(1)
        for i in range(4):
            wc(i, core).start()

    tasks = {
        (0, 3): [q_over_x, lambda: w_hop(1), q_over_y, lambda: w_hop(2)],
        (1, 3): [lambda: w_hop(3), q_over_cores],
        (2, 1): [inputs_here],
        (2, 2): [lambda: w_hop(4), q_done, lambda: left_pair(0)],
        (2, 3): [lambda: left_pair(1)],
        (3, 0): [lambda: left_pair(2)],
        (3, 1): [lambda: left_pair(3)],
        (3, 2): [left_own],
        (3, 3): [left_1, w_middle],
        (4, 2): [left_2],
        (4, 3): [left_3],
        (5, 0): [left_4],
        (5, 1): [left_5],
        (5, 2): [w_cores, p_copy.start],
        (6, 1): [lambda: back_own(0)],
        (6, 2): [lambda: back_own(1)],
        (6, 3): [lambda: back_own(2), lambda: early_sent(), lambda: left_sent()],
        (7, 0): [lambda: back_own(3)],
        (7, 1): [lambda: back_twin(0)],
        (7, 2): [lambda: back_twin(1)],
        (7, 3): [lambda: back_twin(2), lambda: w_sent()],
        (8, 1): [lambda: back_twin(3), ig_copy.start],
    }
    slow = [memory_of, right_0, right_1, right_2, right_3, right_4]
    fast = [memory_of, fast_0, fast_1, fast_2]

    def stages_of(chunk):
        return slow if chunk < FAST else fast

    q_copy = pltpu.make_async_copy(s.qo, qo_hbm, s.local.at[0])
    queue, unsent = [], []

    def early_sent():
        only(0, lambda: qz(0).wait_send())
        only(0, lambda: wz(0).wait_send())
        for i in range(1, 4):
            qz(i).wait_send()
            wz(i).wait_send()
        for d in range(1, NODES):
            a_copy(d, me).wait_send()
        for k in range(1, SIDE):
            qx(k, x).wait_send()
            qy(k, y).wait_send()
        qc(core).wait_send()

    def left_sent():
        lc0(core).wait_send()
        lc1(core).wait_send()
        for d in range(1, NODES):
            lzc(d, me).wait_send()
        for k in range(1, SIDE):
            lxc(k, x).wait_send()
            lyc(k, y).wait_send()

    def w_sent():
        for half in range(2):
            for step in range(2):
                for k in range(1, SIDE):
                    w_step(half, step, k, w_where(half, step)).wait_send()
        for i in range(4):
            wc(i, core).wait_send()

    def g_sent(t):
        for hop in range(4):
            if 0 <= t - hop < CHUNKS:
                for way in range(2):
                    g_copy(way, t - hop, hop).wait_send()

    def right_sent(chunk, stage):
        if chunk < FAST:
            if stage == 1:
                rcc(chunk).wait_send()
            if stage == 4:
                rdc(chunk, core).wait_send()
            for k in range(1, SIDE):
                if stage == 2:
                    rxc(chunk, k, x).wait_send()
                if stage == 3:
                    ryc(chunk, k, y).wait_send()
        else:
            for k in range(1, 2 * SIDE):
                if stage == 1:
                    rfc(chunk, k, place).wait_send()
                if stage == 2 and k < SIDE:
                    rgc(chunk, k, y).wait_send()

    def advance():
        moved = []
        for chunk, stage in queue:
            stages_of(chunk)[stage](chunk)
            unsent.append((chunk, stage))
            if stage + 1 < len(stages_of(chunk)):
                moved.append((chunk, stage + 1))
        queue[:] = moved

    def own(chunk):
        if chunk < CHUNKS:
            for way in range(2):
                g_copy(way, chunk, 0).start()

    qz_start()
    wz_start(0)
    for d in (4, 3, 5, 2, 6, 1, 7):
        a_copy(d, me).start()
    for chunk in range(AHEAD):
        own(chunk)
    for t in range(CHUNKS + 4):
        own(t + AHEAD)
        for hop in range(4):
            chunk = t - hop
            if hop and 0 <= chunk < CHUNKS:
                for way in range(2):
                    g_arrived(way, chunk, hop - 1)
                    g_copy(way, chunk, hop).start()
            for task in tasks.get((t, hop), ()):
                task()
            if 5 <= t < CALM and hop in (2, 3):
                advance()
        if 4 <= t < CHUNKS:
            g_sent(t - 4)
            for chunk, stage in unsent[:-8]:
                right_sent(chunk, stage)
            del unsent[:-8]
        if t == 3:
            start_memory()
        if t >= CALM:
            advance()
        if t >= 4:
            for way in range(2):
                g_arrived(way, t - 4, 3)
            memory_of(t - 4)
            if t >= CALM:
                stages_of(t - 4)[1](t - 4)
                unsent.append((t - 4, 1))
            queue.append((t - 4, 2 if t >= CALM else 1))
    for t in range(CHUNKS - 4, CHUNKS):
        g_sent(t)
    while queue:
        advance()

    q_copy.start()
    for chunk, stage in unsent:
        right_sent(chunk, stage)
    for t in range(CHUNKS, CHUNKS + 4):
        g_sent(t)
    for chunk in range(CHUNKS):
        ne_copy(chunk).wait()
    ig_copy.wait()
    p_copy.wait()
    q_copy.wait()


def shards(attn_out, out_grad, weight, error, q_prev):
    anywhere = pl.BlockSpec(memory_space=pl.ANY)
    input_grad, new_error, p_out, q_out = pl.pallas_call(
        fused_kernel,
        out_shape=(
            jax.ShapeDtypeStruct((TOK, FEATS), BF16),
            jax.ShapeDtypeStruct((SHARD, D), BF16),
            jax.ShapeDtypeStruct((RANK, SHARD), F32),
            jax.ShapeDtypeStruct((RANK, D), F32),
        ),
        in_specs=[anywhere] * 5,
        out_specs=[anywhere] * 4,
        scratch_shapes=list(SCRATCH.values()),
        compiler_params=pltpu.CompilerParams(
            collective_id=0, has_side_effects=True, vmem_limit_bytes=63 * 2**20
        ),
        name="powersgd",
    )(attn_out[0], out_grad[0], weight, error[0], q_prev[0])
    return input_grad[None], new_error[None], p_out, q_out[None]


def solution(mesh):
    in_specs = (
        P("rep", "node", None),
        P("rep", "node", None),
        P("node", None),
        P("rep", "node", None),
        P("node", None, None),
    )
    out_specs = (
        P("rep", "node", None),
        P("rep", "node", None),
        P(None, "node"),
        P("node", None, None),
    )
    return jax.shard_map(shards, mesh=mesh, in_specs=in_specs, out_specs=out_specs, check_vma=False)
```

```python
import types

import jax
import jax.numpy as jnp
from jax import lax
from jax.experimental import pallas as pl
from jax.experimental.pallas import tpu as pltpu
from jax.sharding import PartitionSpec as P

MESH = pl.DeviceIdType.MESH
BF16, F32 = jnp.bfloat16, jnp.float32
NODES = 8
SIDE = 4
REPS = 32
TOK = 320
SHARD = 256
RANK = 32
FEATS = NODES * SHARD
D = 3968
WIDE = 4096
WIDTHS = (768, 768, 640, 640, 512, 384, 128, 128)
STARTS = tuple(sum(WIDTHS[:i]) for i in range(len(WIDTHS)))
CHUNKS = len(WIDTHS)
FAST = 6
FAST_AT = STARTS[FAST]
CALM = CHUNKS - 1
AHEAD = 1
SPLIT = 160

DMA = pltpu.SemaphoreType.DMA
SCRATCH = dict(
    gbuf=pltpu.VMEM((NODES, TOK, D), BF16),
    abuf=pltpu.VMEM((NODES, TOK, SHARD), BF16),
    at=pltpu.VMEM((SHARD, NODES * TOK), BF16),
    avm=pltpu.VMEM((TOK, FEATS), BF16),
    errbuf=pltpu.VMEM((SHARD, D), BF16),
    mem=pltpu.VMEM((SHARD, D), F32),
    wbuf=pltpu.VMEM((NODES, SIDE, SIDE, 16, D), BF16),
    qbuf=pltpu.VMEM((NODES, RANK, WIDE), F32),
    qloc=pltpu.VMEM((RANK, WIDE), F32),
    qsp=pltpu.VMEM((3 * 2 * RANK, D), BF16),
    lbuf=pltpu.VMEM((NODES, RANK, SHARD), F32),
    lrx=pltpu.VMEM((NODES, RANK // 2, SHARD), F32),
    l2=pltpu.VMEM((NODES, RANK // 2, SHARD), F32),
    lz=pltpu.VMEM((NODES, RANK // 2, SHARD), F32),
    lx=pltpu.VMEM((SIDE, RANK // 2, SHARD), F32),
    ly=pltpu.VMEM((SIDE, RANK // 2, SHARD), F32),
    left=pltpu.VMEM((RANK, SHARD), F32),
    basis=pltpu.VMEM((RANK, SHARD), F32),
    b3=pltpu.VMEM((3 * RANK, SHARD), BF16),
    bt6=pltpu.VMEM((SHARD, 6 * RANK), BF16),
    rs=pltpu.VMEM((RANK, D), F32),
    rc=pltpu.VMEM((RANK // 2, D), F32),
    rx=pltpu.VMEM((SIDE, RANK // 2, D), F32),
    ry=pltpu.VMEM((SIDE, RANK // 2, D), F32),
    qo=pltpu.VMEM((RANK, D), F32),
    rf=pltpu.VMEM((2 * SIDE, RANK, D - FAST_AT), F32),
    rg=pltpu.VMEM((SIDE, RANK, D - FAST_AT), F32),
    local=DMA((8,)),
    out=DMA((CHUNKS,)),
    a_s=DMA((NODES,)), a_r=DMA((NODES,)),
    g_s=DMA((2, CHUNKS, 4)), g_r=DMA((2, CHUNKS, 4)),
    qz_s=DMA((4,)), qz_r=DMA((4,)),
    qx_s=DMA((4,)), qx_r=DMA((4,)),
    qy_s=DMA((4,)), qy_r=DMA((4,)),
    qc_s=DMA((1,)), qc_r=DMA((1,)),
    wz_s=DMA((4,)), wz_r=DMA((4,)),
    wx_s=DMA((2, 4)), wx_r=DMA((2, 4)),
    wy_s=DMA((2, 4)), wy_r=DMA((2, 4)),
    wc_s=DMA((4,)), wc_r=DMA((4,)),
    lc_s=DMA((2,)), lc_r=DMA((2,)),
    lz_s=DMA((NODES,)), lz_r=DMA((NODES,)),
    lx_s=DMA((4,)), lx_r=DMA((4,)),
    ly_s=DMA((4,)), ly_r=DMA((4,)),
    rc_s=DMA((CHUNKS,)), rc_r=DMA((CHUNKS,)),
    rd_s=DMA((CHUNKS,)), rd_r=DMA((CHUNKS,)),
    rf_s=DMA((CHUNKS, 8)), rf_r=DMA((CHUNKS, 8)),
    rx_s=DMA((CHUNKS, 4)), rx_r=DMA((CHUNKS, 4)),
    ry_s=DMA((CHUNKS, 4)), ry_r=DMA((CHUNKS, 4)),
)


def split3(value):
    high = value.astype(BF16)
    rest = value - high.astype(F32)
    middle = rest.astype(BF16)
    low = (rest - middle.astype(F32)).astype(BF16)
    return high, middle, low


def dot_nt(a, b):
    return lax.dot_general(a, b, (((1,), (1,)), ((), ())), preferred_element_type=F32)


def dot_nn(a, b):
    return jnp.dot(a, b, preferred_element_type=F32)


def thirds(value, rows):
    return value[:rows] + value[rows : 2 * rows] + value[2 * rows :]


def fused_kernel(
    a_hbm, g_hbm, w_hbm, e_hbm, q_hbm, ig_hbm, ne_hbm, p_hbm, qo_hbm, *scratch
):
    s = types.SimpleNamespace(**dict(zip(SCRATCH, scratch)))
    me = lax.axis_index("node")
    rep = lax.axis_index("rep")
    x = lax.div(rep, 2 * SIDE)
    y = lax.rem(lax.div(rep, 2), SIDE)
    core = lax.rem(rep, 2)
    chip = y * SIDE + x

    def node(d):
        return lax.rem(me + d + 2 * NODES, NODES)

    def along(v, k):
        return lax.rem(v + k + SIDE, SIDE)

    def z_peer(d):
        return {"node": node(d)}

    def x_peer(k):
        return {"rep": along(x, k) * 2 * SIDE + y * 2 + core}

    def y_peer(k):
        return {"rep": x * 2 * SIDE + along(y, k) * 2 + core}

    def pair_peer(k):
        other = lax.rem(x * 2 + core + k, 2 * SIDE)
        return {"rep": lax.div(other, 2) * 2 * SIDE + y * 2 + lax.rem(other, 2)}

    twin = {"rep": x * 2 * SIDE + y * 2 + (1 - core)}

    def remote(src, dst, send_sem, recv_sem, device):
        return pltpu.make_async_remote_copy(
            src_ref=src, dst_ref=dst, send_sem=send_sem, recv_sem=recv_sem,
            device_id=device, device_id_type=MESH,
        )

    def plane_of(slot):
        return lax.rem(me + (jnp.where(slot < 4, 7 - slot, slot - 4)), NODES)

    def part(start, size):
        return pl.ds(pl.multiple_of(start, size), size)

    mine = part(core * 4, 4)
    chip_cols = part(chip * 256, 256)

    barrier = pltpu.get_barrier_semaphore()
    friends = [z_peer(d) for d in range(1, NODES)]
    friends += [pair_peer(k) for k in range(1, 2 * SIDE)] + [y_peer(k) for k in range(1, SIDE)]
    for friend in friends:
        pl.semaphore_signal(barrier, inc=1, device_id=friend, device_id_type=MESH)

    own_q = pltpu.make_async_copy(q_hbm, s.qloc.at[:, pl.ds(0, D)], s.local.at[0])
    own_q.start()
    own_g = pltpu.make_async_copy(g_hbm, s.gbuf.at[me], s.local.at[1])
    own_g.start()
    own_a = pltpu.make_async_copy(a_hbm.at[:, part(me * SHARD, SHARD)], s.abuf.at[me], s.local.at[2])
    own_a.start()
    all_a = pltpu.make_async_copy(a_hbm, s.avm, s.local.at[3])
    all_a.start()
    own_e = pltpu.make_async_copy(e_hbm, s.errbuf, s.local.at[4])
    own_e.start()
    s.qloc[:, D:] = jnp.zeros((RANK, WIDE - D), F32)
    pl.semaphore_wait(barrier, len(friends))
    own_q.wait()

    def qz(i):
        slot = core * 4 + i
        d = jnp.where(core == 0, i + 1, -i)
        return remote(
            s.qloc.at[:, chip_cols], s.qbuf.at[slot, :, chip_cols], s.qz_s.at[i], s.qz_r.at[i], z_peer(d)
        )

    qz_own = pltpu.make_async_copy(s.qloc.at[:, chip_cols], s.qbuf.at[4, :, chip_cols], s.local.at[5])

    def only(which, action):
        pl.when(core == which)(action)

    def qz_start():
        only(0, lambda: qz(0).start())
        only(1, lambda: qz_own.start())
        for i in range(1, 4):
            qz(i).start()

    def qz_wait():
        only(0, lambda: qz(0).wait_recv())
        only(1, lambda: qz_own.wait())
        for i in range(1, 4):
            qz(i).wait_recv()

    def qz_sent():
        only(0, lambda: qz(0).wait_send())
        for i in range(1, 4):
            qz(i).wait_send()

    def qx(k, at):
        region = s.qbuf.at[mine, :, part((y * SIDE + at) * 256, 256)]
        return remote(region, region, s.qx_s.at[k], s.qx_r.at[k], x_peer(k))

    def qy(k, at):
        region = s.qbuf.at[mine, :, part(at * 1024, 1024)]
        return remote(region, region, s.qy_s.at[k], s.qy_r.at[k], y_peer(k))

    def qc(at):
        region = s.qbuf.at[part(at * 4, 4)]
        return remote(region, region, s.qc_s.at[0], s.qc_r.at[0], twin)

    w_rows = w_hbm.at[part(chip * 16, 16)]
    onward = {"node": lax.rem(me + jnp.where(core == 0, 1, NODES - 1), NODES)}

    def wz(i):
        slot = core * 4 + i
        src = w_rows if i == 0 else s.wbuf.at[slot - 1, y, x]
        return remote(src, s.wbuf.at[slot, y, x], s.wz_s.at[i], s.wz_r.at[i], onward)

    wz_own = pltpu.make_async_copy(w_rows, s.wbuf.at[4, y, x], s.local.at[6])

    def wz_start(i):
        if i == 0:
            only(0, lambda: wz(0).start())
            only(1, lambda: wz_own.start())
        else:
            wz(i).start()

    def wz_wait(i):
        if i == 0:
            only(0, lambda: wz(0).wait_recv())
            only(1, lambda: wz_own.wait())
        else:
            wz(i).wait_recv()

    def w_step(half, step, k, at):
        slots = part(core * 4 + 2 * half, 2)
        if (half == 0) == (step == 0):
            if step == 0:
                region = s.wbuf.at[slots, y, at]
            else:
                region = s.wbuf.at[slots, :, at]
            return remote(region, region, s.wx_s.at[half, k], s.wx_r.at[half, k], x_peer(k))
        if step == 0:
            region = s.wbuf.at[slots, at, x]
        else:
            region = s.wbuf.at[slots, at]
        return remote(region, region, s.wy_s.at[half, k], s.wy_r.at[half, k], y_peer(k))

    def w_where(half, step):
        return x if (half == 0) == (step == 0) else y

    def w_start(step):
        for half in range(2):
            for k in range(1, SIDE):
                w_step(half, step, k, w_where(half, step)).start()

    def w_wait(step):
        for half in range(2):
            for k in range(1, SIDE):
                w_step(half, step, k, along(w_where(half, step), -k)).wait_recv()

    def wc(i, at):
        region = s.wbuf.at[at * 4 + i]
        return remote(region, region, s.wc_s.at[i], s.wc_r.at[i], twin)

    def a_copy(d, at):
        to = node(d)
        return remote(a_hbm.at[:, part(to * SHARD, SHARD)], s.abuf.at[at], s.a_s.at[d], s.a_r.at[d], {"node": to})

    def g_copy(way, chunk, hop):
        source = node(-hop if way == 0 else hop)
        if hop < 3:
            rows = pl.ds(0, TOK)
        else:
            rows = pl.ds(0, SPLIT) if way == 0 else pl.ds(SPLIT, TOK - SPLIT)
        cols = pl.ds(STARTS[chunk], WIDTHS[chunk])
        dst = s.gbuf.at[source, rows, cols]
        src = g_hbm.at[:, cols] if hop == 0 else dst
        return remote(
            src, dst, s.g_s.at[way, chunk, hop], s.g_r.at[way, chunk, hop], z_peer(1 if way == 0 else -1)
        )

    def g_arrived(way, chunk, hop):
        source = node(-hop - 1 if way == 0 else hop + 1)
        if hop < 3:
            rows = pl.ds(0, TOK)
        else:
            rows = pl.ds(0, SPLIT) if way == 0 else pl.ds(SPLIT, TOK - SPLIT)
        region = s.gbuf.at[source, rows, pl.ds(STARTS[chunk], WIDTHS[chunk])]
        remote(
            region, region, s.g_s.at[way, chunk, hop], s.g_r.at[way, chunk, hop], z_peer(1 if way == 0 else -1)
        ).wait_recv()

    def inputs_here():
        own_g.wait()
        all_a.wait()
        own_e.wait()

    def left_pair(half):
        for i in range(2):
            pieces = split3(s.qbuf[2 * half + i, :, pl.ds(0, D)])
            for j in range(3):
                s.qsp[pl.ds(64 * j + 32 * i, RANK), :] = pieces[j]
        pieces = split3(thirds(dot_nt(s.qsp[...], s.gbuf[me]), 2 * RANK))
        for i in range(2):
            plane = plane_of(2 * half + i)
            stacked = jnp.concatenate([piece[RANK * i : RANK * (i + 1)] for piece in pieces], axis=0)
            s.lbuf[plane] = thirds(dot_nn(stacked, s.avm[:, part(plane * SHARD, SHARD)]), RANK)

    def left_own():
        pieces = split3(s.qloc[:, pl.ds(0, D)])
        s.lbuf[me] += thirds(dot_nt(jnp.concatenate(pieces, axis=0), s.errbuf[...]), RANK)
        lc0(core).start()

    def lc0(at):
        return remote(
            s.lbuf.at[:, part((1 - at) * 16, 16)], s.lrx, s.lc_s.at[0], s.lc_r.at[0], twin
        )

    def lzc(d, at):
        to = node(d)
        return remote(s.l2.at[to], s.lz.at[at], s.lz_s.at[d], s.lz_r.at[d], {"node": to})

    def lxc(k, at):
        return remote(s.lx.at[at], s.lx.at[at], s.lx_s.at[k], s.lx_r.at[k], x_peer(k))

    def lyc(k, at):
        return remote(s.ly.at[at], s.ly.at[at], s.ly_s.at[k], s.ly_r.at[k], y_peer(k))

    def lc1(at):
        region = s.left.at[part(at * 16, 16)]
        return remote(region, region, s.lc_s.at[1], s.lc_r.at[1], twin)

    def left_1():
        lc0(core).wait_recv()
        s.l2[...] = s.lbuf[:, part(core * 16, 16), :] + s.lrx[...]
        for d in range(1, NODES):
            lzc(d, me).start()
        s.lz[me] = s.l2[me]

    def added(ref, count):
        total = ref[0]
        for i in range(1, count):
            total = total + ref[i]
        return total

    def left_2():
        for d in range(1, NODES):
            lzc(d, node(-d)).wait_recv()
        s.lx[x] = added(s.lz, NODES)
        for k in range(1, SIDE):
            lxc(k, x).start()

    def left_3():
        for k in range(1, SIDE):
            lxc(k, along(x, -k)).wait_recv()
        s.ly[y] = added(s.lx, SIDE)
        for k in range(1, SIDE):
            lyc(k, y).start()

    def left_4():
        for k in range(1, SIDE):
            lyc(k, along(y, -k)).wait_recv()
        s.left[part(core * 16, 16), :] = added(s.ly, SIDE)
        lc1(core).start()

    def left_5():
        lc1(1 - core).wait_recv()
        left = s.left[...]
        gram = lax.dot_general(
            left, left, (((1,), (1,)), ((), ())), precision=lax.Precision.HIGHEST, preferred_element_type=F32
        )
        row_g = lax.broadcasted_iota(jnp.int32, (RANK, RANK), 0)
        col_g = lax.broadcasted_iota(jnp.int32, (RANK, RANK), 1)
        row_l = lax.broadcasted_iota(jnp.int32, (RANK, SHARD), 0)
        row_1 = lax.broadcasted_iota(jnp.int32, (RANK, 1), 0)

        def step(k, carry):
            gram, left = carry
            column = jnp.sum(jnp.where(col_g == k, gram, 0.0), axis=1, keepdims=True)
            pivot = jnp.sum(jnp.where(row_1 == k, column, 0.0), axis=0, keepdims=True)
            scale = 1.0 / jnp.sqrt(pivot)
            top_g = jnp.sum(jnp.where(row_g == k, gram, 0.0), axis=0, keepdims=True) * scale
            top_l = jnp.sum(jnp.where(row_l == k, left, 0.0), axis=0, keepdims=True) * scale
            below = jnp.where(row_1 > k, column * scale, 0.0)
            gram = jnp.where(row_g == k, top_g, gram - below * top_g)
            left = jnp.where(row_l == k, top_l, left - below * top_l)
            return gram, left

        _, basis = lax.fori_loop(0, RANK, step, (gram, left))
        s.basis[...] = basis
        high, middle, low = split3(basis)
        s.b3[...] = jnp.concatenate([high, middle, low], axis=0)
        s.bt6[...] = jnp.concatenate([basis, basis, middle.astype(F32), middle.astype(F32), high.astype(F32), low.astype(F32)], axis=0).T.astype(BF16)

    p_copy = pltpu.make_async_copy(s.basis, p_hbm, s.local.at[7])

    def cols_of(chunk):
        return pl.ds(STARTS[chunk], WIDTHS[chunk])

    def start_memory():
        own_a.wait()
        for d in range(1, NODES):
            a_copy(d, node(-d)).wait_recv()
        s.at[...] = s.abuf[...].reshape(NODES * TOK, SHARD).T

    def memory_of(chunk):
        cols = cols_of(chunk)
        block = s.gbuf[:, :, cols].reshape(NODES * TOK, WIDTHS[chunk])
        s.mem[:, cols] = dot_nn(s.at[...], block) + s.errbuf[:, cols].astype(F32)

    def rcc(chunk):
        cols = cols_of(chunk)
        other = part((1 - core) * 16, 16)
        return remote(s.rs.at[other, cols], s.rc.at[:, cols], s.rc_s.at[chunk], s.rc_r.at[chunk], twin)

    def rdc(chunk, at):
        region = s.qo.at[part(at * 16, 16), cols_of(chunk)]
        return remote(region, region, s.rd_s.at[chunk], s.rd_r.at[chunk], twin)

    def rxc(chunk, k, at):
        region = s.rx.at[at, :, cols_of(chunk)]
        return remote(region, region, s.rx_s.at[chunk, k], s.rx_r.at[chunk, k], x_peer(k))

    def ryc(chunk, k, at):
        region = s.ry.at[at, :, cols_of(chunk)]
        return remote(region, region, s.ry_s.at[chunk, k], s.ry_r.at[chunk, k], y_peer(k))

    def right_local(chunk):
        cols = cols_of(chunk)
        high, middle, low = split3(s.mem[:, cols])
        total = thirds(dot_nn(s.b3[...], high), RANK)
        second = dot_nn(s.b3[: 2 * RANK], middle)
        return total + (second[:RANK] + second[RANK:]) + dot_nn(s.b3[:RANK], low)

    def right_0(chunk):
        s.rs[:, cols_of(chunk)] = right_local(chunk)
        rcc(chunk).start()

    def right_1(chunk):
        cols = cols_of(chunk)
        rcc(chunk).wait_recv()
        s.rx[x, :, cols] = s.rs[part(core * 16, 16), cols] + s.rc[:, cols]
        for k in range(1, SIDE):
            rxc(chunk, k, x).start()

    def right_2(chunk):
        cols = cols_of(chunk)
        for k in range(1, SIDE):
            rxc(chunk, k, along(x, -k)).wait_recv()
        s.ry[y, :, cols] = ((s.rx[0, :, cols] + s.rx[1, :, cols]) + s.rx[2, :, cols]) + s.rx[3, :, cols]
        for k in range(1, SIDE):
            ryc(chunk, k, y).start()

    def ne_copy(chunk):
        cols = cols_of(chunk)
        return pltpu.make_async_copy(s.errbuf.at[:, cols], ne_hbm.at[:, cols], s.out.at[chunk])

    def right_3(chunk):
        cols = cols_of(chunk)
        for k in range(1, SIDE):
            ryc(chunk, k, along(y, -k)).wait_recv()
        total = ((s.ry[0, :, cols] + s.ry[1, :, cols]) + s.ry[2, :, cols]) + s.ry[3, :, cols]
        s.qo[part(core * 16, 16), cols] = total * (1.0 / REPS)
        rdc(chunk, core).start()

    def right_4(chunk):
        cols = cols_of(chunk)
        rdc(chunk, 1 - core).wait_recv()
        finish(chunk, s.qo[:, cols])

    def finish(chunk, right):
        cols = cols_of(chunk)
        high, middle, low = split3(right)
        approx = dot_nn(s.bt6[...], jnp.concatenate([high, middle, high, middle, low, high], axis=0))
        s.errbuf[:, cols] = (s.mem[:, cols] - approx).astype(BF16)
        ne_copy(chunk).start()

    def short(chunk):
        return pl.ds(STARTS[chunk] - FAST_AT, WIDTHS[chunk])

    place = x * 2 + core

    def rfc(chunk, k, at):
        region = s.rf.at[at, :, short(chunk)]
        return remote(region, region, s.rf_s.at[chunk, k], s.rf_r.at[chunk, k], pair_peer(k))

    def rgc(chunk, k, at):
        region = s.rg.at[at, :, short(chunk)]
        return remote(region, region, s.ry_s.at[chunk, k], s.ry_r.at[chunk, k], y_peer(k))

    def fast_0(chunk):
        s.rf[place, :, short(chunk)] = right_local(chunk)
        for k in range(1, 2 * SIDE):
            rfc(chunk, k, place).start()

    def fast_1(chunk):
        for k in range(1, 2 * SIDE):
            rfc(chunk, k, lax.rem(place + 2 * SIDE - k, 2 * SIDE)).wait_recv()
        total = s.rf[0, :, short(chunk)]
        for i in range(1, 2 * SIDE):
            total = total + s.rf[i, :, short(chunk)]
        s.rg[y, :, short(chunk)] = total
        for k in range(1, SIDE):
            rgc(chunk, k, y).start()

    def fast_2(chunk):
        for k in range(1, SIDE):
            rgc(chunk, k, along(y, -k)).wait_recv()
        total = s.rg[0, :, short(chunk)]
        for i in range(1, SIDE):
            total = total + s.rg[i, :, short(chunk)]
        right = total * (1.0 / REPS)
        s.qo[:, cols_of(chunk)] = right
        finish(chunk, right)

    def back(slot):
        plane = plane_of(slot)
        block = s.wbuf[slot].reshape(SHARD, D)
        s.avm[:, part(plane * SHARD, SHARD)] = dot_nt(s.gbuf[me], block).astype(BF16)

    def back_own(i):
        back(core * 4 + i)

    def back_twin(i):
        wc(i, 1 - core).wait_recv()
        back((1 - core) * 4 + i)

    ig_copy = pltpu.make_async_copy(s.avm, ig_hbm, s.local.at[3])

    def q_over_x():
        qz_wait()
        for k in range(1, SIDE):
            qx(k, x).start()

    def q_over_y():
        for k in range(1, SIDE):
            qx(k, along(x, -k)).wait_recv()
        for k in range(1, SIDE):
            qy(k, y).start()

    def q_over_cores():
        for k in range(1, SIDE):
            qy(k, along(y, -k)).wait_recv()
        qc(core).start()

    def q_done():
        qc(1 - core).wait_recv()

    def w_hop(i):
        wz_wait(i - 1)
        if i < 4:
            wz_start(i)
        else:
            w_start(0)

    def w_middle():
        w_wait(0)
        w_start(1)

    def w_cores():
        w_wait(1)
        for i in range(4):
            wc(i, core).start()

    tasks = {
        (0, 3): [q_over_x, lambda: w_hop(1), q_over_y, lambda: w_hop(2)],
        (1, 3): [lambda: w_hop(3), q_over_cores],
        (2, 1): [inputs_here],
        (2, 2): [lambda: w_hop(4), q_done, lambda: left_pair(0)],
        (2, 3): [lambda: left_pair(1)],
        (3, 0): [lambda: left_pair(2)],
        (3, 1): [lambda: left_pair(3)],
        (3, 2): [left_own],
        (3, 3): [left_1, w_middle],
        (4, 2): [left_2],
        (4, 3): [left_3],
        (5, 0): [left_4],
        (5, 1): [left_5],
        (5, 2): [w_cores, p_copy.start],
        (6, 1): [lambda: back_own(0)],
        (6, 2): [lambda: back_own(1)],
        (6, 3): [lambda: back_own(2), lambda: early_sent(), lambda: left_sent()],
        (7, 0): [lambda: back_own(3)],
        (7, 1): [lambda: back_twin(0)],
        (7, 2): [lambda: back_twin(1)],
        (7, 3): [lambda: back_twin(2), lambda: back_twin(3), ig_copy.start, lambda: w_sent()],
    }
    slow = [memory_of, right_0, right_1, right_2, right_3, right_4]
    fast = [memory_of, fast_0, fast_1, fast_2]

    def stages_of(chunk):
        return slow if chunk < FAST else fast

    q_copy = pltpu.make_async_copy(s.qo, qo_hbm, s.local.at[0])
    queue, unsent = [], []

    def early_sent():
        only(0, lambda: qz(0).wait_send())
        only(0, lambda: wz(0).wait_send())
        for i in range(1, 4):
            qz(i).wait_send()
            wz(i).wait_send()
        for d in range(1, NODES):
            a_copy(d, me).wait_send()
        for k in range(1, SIDE):
            qx(k, x).wait_send()
            qy(k, y).wait_send()
        qc(core).wait_send()

    def left_sent():
        lc0(core).wait_send()
        lc1(core).wait_send()
        for d in range(1, NODES):
            lzc(d, me).wait_send()
        for k in range(1, SIDE):
            lxc(k, x).wait_send()
            lyc(k, y).wait_send()

    def w_sent():
        for half in range(2):
            for step in range(2):
                for k in range(1, SIDE):
                    w_step(half, step, k, w_where(half, step)).wait_send()
        for i in range(4):
            wc(i, core).wait_send()

    def g_sent(t):
        for hop in range(4):
            if 0 <= t - hop < CHUNKS:
                for way in range(2):
                    g_copy(way, t - hop, hop).wait_send()

    def right_sent(chunk, stage):
        if chunk < FAST:
            if stage == 1:
                rcc(chunk).wait_send()
            if stage == 4:
                rdc(chunk, core).wait_send()
            for k in range(1, SIDE):
                if stage == 2:
                    rxc(chunk, k, x).wait_send()
                if stage == 3:
                    ryc(chunk, k, y).wait_send()
        else:
            for k in range(1, 2 * SIDE):
                if stage == 1:
                    rfc(chunk, k, place).wait_send()
                if stage == 2 and k < SIDE:
                    rgc(chunk, k, y).wait_send()

    def advance():
        moved = [(chunk, stage) for chunk, stage in queue if stage + 1 < len(stages_of(chunk))]
        last = [(chunk, stage) for chunk, stage in queue if stage + 1 == len(stages_of(chunk))]
        for chunk, stage in moved + last:
            stages_of(chunk)[stage](chunk)
            unsent.append((chunk, stage))
        queue[:] = [(chunk, stage + 1) for chunk, stage in moved]

    def own(chunk):
        if chunk < CHUNKS:
            for way in range(2):
                g_copy(way, chunk, 0).start()

    qz_start()
    wz_start(0)
    for d in (4, 3, 5, 2, 6, 1, 7):
        a_copy(d, me).start()
    for chunk in range(AHEAD):
        own(chunk)
    for t in range(CHUNKS + 4):
        own(t + AHEAD)
        for hop in range(4):
            chunk = t - hop
            if hop and 0 <= chunk < CHUNKS:
                for way in range(2):
                    g_arrived(way, chunk, hop - 1)
                    g_copy(way, chunk, hop).start()
            for task in tasks.get((t, hop), ()):
                task()
            if 5 <= t < CALM and hop in (2, 3):
                advance()
            if t >= CALM and hop and queue:
                chunk, stage = queue.pop(0)
                stages_of(chunk)[stage](chunk)
                unsent.append((chunk, stage))
                if stage + 1 < len(stages_of(chunk)):
                    queue.append((chunk, stage + 1))
        if 4 <= t < CHUNKS:
            g_sent(t - 4)
            for chunk, stage in unsent[:-8]:
                right_sent(chunk, stage)
            del unsent[:-8]
        if t == 3:
            start_memory()
        if t >= 4:
            for way in range(2):
                g_arrived(way, t - 4, 3)
            memory_of(t - 4)
            if t >= CALM:
                stages_of(t - 4)[1](t - 4)
                unsent.append((t - 4, 1))
            queue.append((t - 4, 2 if t >= CALM else 1))
    for t in range(CHUNKS - 4, CHUNKS):
        g_sent(t)
    while queue:
        advance()

    q_copy.start()
    for chunk, stage in unsent:
        right_sent(chunk, stage)
    for t in range(CHUNKS, CHUNKS + 4):
        g_sent(t)
    for chunk in range(CHUNKS):
        ne_copy(chunk).wait()
    ig_copy.wait()
    p_copy.wait()
    q_copy.wait()


def shards(attn_out, out_grad, weight, error, q_prev):
    anywhere = pl.BlockSpec(memory_space=pl.ANY)
    input_grad, new_error, p_out, q_out = pl.pallas_call(
        fused_kernel,
        out_shape=(
            jax.ShapeDtypeStruct((TOK, FEATS), BF16),
            jax.ShapeDtypeStruct((SHARD, D), BF16),
            jax.ShapeDtypeStruct((RANK, SHARD), F32),
            jax.ShapeDtypeStruct((RANK, D), F32),
        ),
        in_specs=[anywhere] * 5,
        out_specs=[anywhere] * 4,
        scratch_shapes=list(SCRATCH.values()),
        compiler_params=pltpu.CompilerParams(
            collective_id=0, has_side_effects=True, vmem_limit_bytes=63 * 2**20
        ),
        name="powersgd",
    )(attn_out[0], out_grad[0], weight, error[0], q_prev[0])
    return input_grad[None], new_error[None], p_out, q_out[None]


def solution(mesh):
    in_specs = (
        P("rep", "node", None),
        P("rep", "node", None),
        P("node", None),
        P("rep", "node", None),
        P("node", None, None),
    )
    out_specs = (
        P("rep", "node", None),
        P("rep", "node", None),
        P(None, "node"),
        P("node", None, None),
    )
    return jax.shard_map(shards, mesh=mesh, in_specs=in_specs, out_specs=out_specs, check_vma=False)
```
